32 devices in a mesh: row: 4 (over y, x), col: 8 (over z, core).
Axes of the slice: x: 2, y: 2, z: 4, core: 2. Of those that a mesh axis runs over, the one named last changes fastest.
Arguments:
- factors: bfloat16 [16384, 2048], P(('row', 'col')), may hold values from -6 to 6
- dressed: bfloat16 [16384, 2048], P(('col', 'row')), may hold values from -0.125 to 0.125
- amplitudes: float32 [544, 512, 512], P(('row', 'col')), may hold values from -2.4 to 2.4
- fock_vv: float32 [512, 512], replicated, as said below
- occ_energy: float32 [32], replicated, may hold values from -2 to -0.3
- pair_list: int32 [528, 2], replicated, may hold values from 0 to 31, as said below
- owner_map: int32 [528], replicated, may hold values from 0 to 31, as said below
Outputs:
- updated: float32 [544, 512, 512], P(('row', 'col'))
- pair_energy: float32 [544], P(('row', 'col'))
The draws below stay inside these ranges and needn't reach their ends.
Inputs may be any that keep to these rules, and one draw needn't show every extreme that they name: `pair_list`: every unordered pair of occupied orbitals appears exactly once, as i <= j. `owner_map`: each device owns 528 // 32 or 17 pairs, and some device owns exactly 17. `fock_vv`: Symmetric; its diagonal lies between 1 and 3.
All inputs are finite; a program needn't handle non-finite values.
Results may differ from the reference program's by a relative error of at most 0.0041.
Values may be sent and summed in bfloat16 or wider, within the bound.
A program may use at most 192 MiB of HBM per device.

```python
import jax
import jax.numpy as jnp
from jax import lax

O = 32
V = 512
NAUX = 2048
NDEV = 32
NP = 16384
PAIRS = 528
CAP = 17


def draw_fock_vv(key, part):
    level = jax.random.uniform(jax.random.fold_in(key, 5), (V,), jnp.float32, 1.0, 3.0)
    noise = jax.random.normal(jax.random.fold_in(key, 6), (V, V), jnp.float32)
    spread = 0.5 / jnp.sqrt(jnp.float32(V))
    coupling = (noise + noise.T) * spread
    coupling = coupling * (1.0 - jnp.eye(V, dtype=jnp.float32))
    return coupling + jnp.diag(level)


def draw_pair_list(key, part):
    upper = jnp.triu(jnp.ones((O, O), jnp.int32))
    first_orbs, second_orbs = jnp.nonzero(upper, size=PAIRS)
    order = jax.random.permutation(jax.random.fold_in(key, 3), PAIRS)
    return jnp.stack([first_orbs[order], second_orbs[order]], axis=1).astype(jnp.int32)


def draw_owner_map(key, part):
    order = jax.random.permutation(jax.random.fold_in(key, 7), PAIRS)
    devices = jax.random.permutation(jax.random.fold_in(key, 11), NDEV)
    return devices[order % NDEV].astype(jnp.int32)


def block_scale(key, shape, cuts, low, top_value):
    level = 1.0
    for position, blocks in cuts:
        draws = jax.random.uniform(jax.random.fold_in(jax.random.fold_in(key, 6), position), (blocks,), jnp.float32, low / len(cuts), top_value / len(cuts))
        level = level * jnp.repeat(jnp.exp(draws), shape[position] // blocks).reshape((-1,) + (1,) * (len(shape) - 1 - position))
    return level


def normal_values(rng, extent, deviation, limit, pieces=(), held_as=jnp.bfloat16):
    values = jax.random.normal(rng, extent, jnp.float32) * deviation
    if len(pieces) > 0:
        values = block_scale(rng, extent, pieces, -0.22, 0.18) * values
    return jnp.clip(values, min=-limit, max=limit).astype(held_as)


def setup_inputs(seed: int = 0) -> dict:
    key_list = jax.random.split(jax.random.key(seed), 8)
    return {
        "factors": normal_values(key_list[0], (NP, NAUX), 1.0, 6.0, ((0, 32),)),
        "dressed": normal_values(key_list[1], (NP, NAUX), NAUX ** -0.5, 0.125, ((0, 32),)),
        "amplitudes": normal_values(key_list[2], (NDEV * CAP, V, V), 0.3, 2.4, ((0, 32),), jnp.float32),
        "fock_vv": draw_fock_vv(jax.random.fold_in(key_list[7], 71), 0),
        "occ_energy": jnp.clip(jax.random.uniform(key_list[4], (O,), jnp.float32, -2.0, -0.3), -2.0, -0.3),
        "pair_list": draw_pair_list(jax.random.fold_in(key_list[7], 71), 0),
        "owner_map": draw_owner_map(jax.random.fold_in(key_list[7], 71), 0),
    }


def reference(factors, dressed, amplitudes, fock_vv, occ_energy, pair_list, owner_map):
    highest = lax.Precision.HIGHEST
    orbital_level = jnp.diagonal(fock_vv)
    positions = jnp.arange(PAIRS, dtype=jnp.int32)
    same_owner = owner_map[:, None] == owner_map[None, :]
    earlier = positions[:, None] > positions[None, :]
    slot_index = jnp.sum((same_owner & earlier).astype(jnp.int32), axis=1)
    target = (owner_map * CAP + slot_index).astype(jnp.int32)

    def one_pair(inputs):
        pair_row, slot_at = inputs
        first_orb = pair_row[0]
        second_orb = pair_row[1]
        left_first = lax.dynamic_slice_in_dim(factors, (first_orb * V).astype(jnp.int32), V, 0)
        left_second = lax.dynamic_slice_in_dim(factors, (second_orb * V).astype(jnp.int32), V, 0)
        right_first = lax.dynamic_slice_in_dim(dressed, (first_orb * V).astype(jnp.int32), V, 0)
        right_second = lax.dynamic_slice_in_dim(dressed, (second_orb * V).astype(jnp.int32), V, 0)
        forward = jnp.dot(left_first, right_second.T, preferred_element_type=jnp.float32)
        backward = jnp.dot(left_second, right_first.T, preferred_element_type=jnp.float32)
        equal = first_orb == second_orb
        diagonal_part = 0.5 * (forward + forward.T)
        upper = jnp.where(equal, diagonal_part, forward).astype(jnp.bfloat16)
        lower = jnp.where(equal, diagonal_part, backward.T).astype(jnp.bfloat16)
        symmetric = (upper.astype(jnp.float32) + lower.astype(jnp.float32)).astype(jnp.bfloat16)
        source_part = symmetric.astype(jnp.float32)
        current = lax.dynamic_index_in_dim(amplitudes, slot_at, 0, keepdims=False)
        pair_shift = occ_energy[first_orb] + occ_energy[second_orb]
        residual = source_part + jnp.dot(fock_vv, current, precision=highest) + jnp.dot(current, fock_vv, precision=highest) - pair_shift * current
        denominator = orbital_level[:, None] + orbital_level[None, :] - pair_shift
        updated = current - residual / denominator
        energy = jnp.mean(source_part * updated)
        return updated, energy

    new_tiles, energies = lax.map(one_pair, (pair_list, target))
    updated = jnp.zeros((NDEV * CAP, V, V), jnp.float32).at[target].set(new_tiles)
    pair_energy = jnp.zeros((NDEV * CAP,), jnp.float32).at[target].set(energies)
    return updated, pair_energy
```

```python
import functools

import jax
import jax.numpy as jnp
from jax import lax
from jax.experimental import pallas as pl
from jax.experimental.pallas import tpu as pltpu
from jax.sharding import PartitionSpec as P

MESH = pl.DeviceIdType.MESH
MIB = 1024 * 1024


def split_axis(size):
    return (size // 2, 2) if size % 2 == 0 else (size, 1)


def when(conds, body):
    if not conds:
        body()
        return
    total = conds[0]
    for extra in conds[1:]:
        total = jnp.logical_and(total, extra)
    pl.when(total)(body)


def neighbours(position, size):
    if size == 1:
        return []
    if size == 2:
        return [(0, 1 - position, [])]
    return [
        (0, position + 1, [position + 1 < size]),
        (1, position - 1, [position >= 1]),
    ]


def arrivals(position, size, step):
    if size == 2:
        return [(1 - position, None, [])]
    return [
        (position - step, 0, [position - step >= 0]),
        (position + step, 1, [position + step < size]),
    ]


def gather_kernel(row_count, col_count, left_ref, right_ref, left_all, right_all, send_sem, recv_sem, own_sem):
    highs, lows = split_axis(row_count)
    lines, cores = split_axis(col_count)
    row, col = lax.axis_index("row"), lax.axis_index("col")
    high, low = row // lows, row % lows
    line, core = col // cores, col % cores
    place = {"line": line, "low": low, "high": high, "core": core}
    extent = {"line": lines, "low": lows, "high": highs, "core": cores}
    arrays = (
        (left_ref, left_all, ("line", "low", "high")),
        (right_ref, right_all, ("line", "high", "low")),
    )

    def device(at):
        return (at["high"] * lows + at["low"], at["line"] * cores + at["core"])

    def block_of(which, at):
        r, c = device(at)
        return r * col_count + c if which == 0 else c * row_count + r

    barrier = pltpu.get_barrier_semaphore()
    for axis in ("line", "low", "high", "core"):
        for _, other, conds in neighbours(place[axis], extent[axis]):
            when(conds, lambda axis=axis, other=other: pl.semaphore_signal(
                barrier, inc=1, device_id=device({**place, axis: other}), device_id_type=MESH))
    peers = 0
    for axis in ("line", "low", "high", "core"):
        for _, other, conds in neighbours(place[axis], extent[axis]):
            peers += conds[0].astype(jnp.int32) if conds else 1
    pl.semaphore_wait(barrier, peers)

    sent = []

    def plan(which, origin, stage, travel, guard, own=False):
        source, target, order = arrays[which]
        hops = []
        for later in range(stage, len(order)):
            axis = order[later]
            for way, other, conds in neighbours(place[axis], extent[axis]):
                if later == stage and not own and (extent[axis] == 2 or way != travel):
                    continue
                hops.append((axis, 2 * later + way, other, conds))
        for _, other, conds in neighbours(core, cores):
            hops.append(("core", 6, other, conds))
        copies = []
        for axis, lane, other, conds in hops:
            def make(axis=axis, lane=lane, other=other):
                blk = block_of(which, origin)
                return pltpu.make_async_remote_copy(
                    src_ref=source if own else target.at[blk],
                    dst_ref=target.at[blk],
                    send_sem=send_sem.at[which, blk, lane],
                    recv_sem=recv_sem.at[which, blk],
                    device_id=device({**place, axis: other}),
                    device_id_type=MESH,
                )

            copies.append((conds, make))
            sent.append((guard + conds, make))
        return copies

    def arrived(which, blk):
        target = arrays[which][1]
        pltpu.make_async_remote_copy(
            src_ref=target.at[blk], dst_ref=target.at[blk],
            send_sem=send_sem.at[which, blk, 0], recv_sem=recv_sem.at[which, blk],
            device_id=device(place), device_id_type=MESH,
        ).wait_recv()

    own_copies = []
    for which in range(2):
        for conds, make in plan(which, place, 0, None, [], own=True):
            when(conds, lambda: make().start())
        source, target, _ = arrays[which]
        copy = pltpu.make_async_copy(source, target.at[block_of(which, place)], own_sem.at[which])
        copy.start()
        own_copies.append(copy)

    def take(which, origin, stage, travel, guard):
        copies = plan(which, origin, stage, travel, guard)

        def body():
            arrived(which, block_of(which, origin))
            for conds, make in copies:
                when(conds, lambda: make().start())

        when(guard, body)

    def distance(step):
        if step == 0:
            return [(line, None, [])]
        return arrivals(line, lines, step)

    for turn in range(lines + 2):
        if 1 <= turn < lines:
            for origin, travel, guard in distance(turn):
                for which in range(2):
                    take(which, {**place, "line": origin}, 0, travel, guard)
        if 0 <= turn - 1 < lines:
            for from_line, _, guard in distance(turn - 1):
                for step in range(1, max(highs, lows)):
                    for which in range(2):
                        axis = arrays[which][2][1]
                        if step >= extent[axis]:
                            continue
                        for origin, travel, more in arrivals(place[axis], extent[axis], step):
                            take(which, {**place, "line": from_line, axis: origin}, 1, travel, guard + more)
        if 0 <= turn - 2 < lines:
            for from_line, _, guard in distance(turn - 2):
                for offset in range(max(highs, lows)):
                    for step in range(1, max(highs, lows)):
                        for which in range(2):
                            first, last = arrays[which][2][1:]
                            if offset >= extent[first] or step >= extent[last]:
                                continue
                            shifted = (place[first] + offset) % extent[first]
                            for origin, travel, more in arrivals(place[last], extent[last], step):
                                take(which, {**place, "line": from_line, first: shifted, last: origin}, 2, travel, guard + more)

    if cores > 1:
        def from_sibling(index, carry):
            at = {
                "high": index // (lows * lines),
                "low": index // lines % lows,
                "line": index % lines,
                "core": 1 - core,
            }
            for which in range(2):
                arrived(which, block_of(which, at))
            return carry

        lax.fori_loop(0, highs * lows * lines, from_sibling, 0)
    for conds, make in sent:
        when(conds, lambda: make().wait_send())
    for copy in own_copies:
        copy.wait()


def gather(factors, dressed):
    row_count, col_count = lax.axis_size("row"), lax.axis_size("col")
    devices = row_count * col_count
    rows, depth = factors.shape
    whole = jax.ShapeDtypeStruct((devices, rows, depth), factors.dtype)
    return pl.pallas_call(
        functools.partial(gather_kernel, row_count, col_count),
        out_shape=(whole, whole),
        in_specs=[pl.BlockSpec(memory_space=pl.ANY)] * 2,
        out_specs=(pl.BlockSpec(memory_space=pl.ANY), pl.BlockSpec(memory_space=pl.ANY)),
        scratch_shapes=[
            pltpu.SemaphoreType.DMA((2, devices, 7)),
            pltpu.SemaphoreType.DMA((2, devices)),
            pltpu.SemaphoreType.DMA((2,)),
        ],
        compiler_params=pltpu.CompilerParams(
            collective_id=0, has_side_effects=True, vmem_limit_bytes=4 * MIB
        ),
    )(factors, dressed)


def products(l_i, y_j, y_i, l_j):
    contract = (((1,), (1,)), ((), ()))
    forward = lax.dot_general(l_i[0], y_j[0], contract, preferred_element_type=jnp.float32)
    backward = lax.dot_general(y_i[0], l_j[0], contract, preferred_element_type=jnp.float32)
    return forward, backward


def partial_kernel(first, second, live, shift, l_i, y_j, y_i, l_j, sums):
    forward, backward = products(l_i, y_j, y_i, l_j)
    sums[0, 0] = forward
    sums[0, 1] = backward


def pair_kernel(earlier, first, second, live, shift, l_i, y_j, y_i, l_j, amp, coupling, level_col, level_row, *rest):
    out, energy = rest[earlier:]
    slot = pl.program_id(0)
    forward, backward = products(l_i, y_j, y_i, l_j)
    for sums in rest[:earlier]:
        forward = forward + sums[0, 0]
        backward = backward + sums[0, 1]
    apart = forward.astype(jnp.bfloat16).astype(jnp.float32) + backward.astype(jnp.bfloat16).astype(jnp.float32)
    same = first[slot] == second[slot]
    source = jnp.where(same, forward + backward, apart).astype(jnp.bfloat16).astype(jnp.float32)
    current = amp[0].astype(jnp.bfloat16)
    mixed = jnp.dot(coupling[...], current, preferred_element_type=jnp.float32)
    mixed = mixed + jnp.dot(current, coupling[...], preferred_element_type=jnp.float32)
    denominator = level_col[...] + level_row[...] - shift[slot]
    updated = jnp.where(live[slot] > 0, -(source + mixed) / denominator, 0.0)
    out[0] = updated
    total = jnp.sum(source * updated) / (updated.shape[0] * updated.shape[1])
    energy[...] = jnp.full(energy.shape, total, jnp.float32)


def local(factors, dressed, amplitudes, fock_vv, occ_energy, pair_list, owner_map):
    col_count = lax.axis_size("col")
    capacity = amplitudes.shape[0]
    virtual = fock_vv.shape[0]
    occupied = occ_energy.shape[0]
    depth = factors.shape[1]
    passes = 1 if lax.axis_size("row") * col_count <= 32 else 2
    depth = depth // passes

    own_index = lax.axis_index("row") * col_count + lax.axis_index("col")
    positions = jnp.arange(pair_list.shape[0], dtype=jnp.int32)
    mine = owner_map == own_index
    rank = jnp.sum((mine[None, :] & (positions[:, None] > positions[None, :])).astype(jnp.int32), axis=1)
    hit = mine[None, :] & (rank[None, :] == jnp.arange(capacity, dtype=jnp.int32)[:, None])
    live = jnp.sum(hit.astype(jnp.int32), axis=1)
    pair_orbs = jnp.sum(jnp.where(hit[:, :, None], pair_list[None, :, :], 0), axis=1)
    first, second = pair_orbs[:, 0], pair_orbs[:, 1]
    shift = occ_energy[first] + occ_energy[second]

    level = jnp.diagonal(fock_vv)
    off = jnp.where(jnp.eye(virtual, dtype=jnp.bool_), 0.0, fock_vv).astype(jnp.bfloat16)

    def panel(pick):
        return pl.BlockSpec((1, virtual, depth), lambda s, f, g, *_: ((f, g)[pick][s], 0, 0))

    def fixed(*shape):
        return pl.BlockSpec(shape, lambda s, *_: (0,) * len(shape))

    def per_slot(*shape):
        return pl.BlockSpec((1,) + shape, lambda s, *_: (s,) + (0,) * len(shape))

    def run(kernel, panels, others, other_specs, out_shape, out_specs):
        return pl.pallas_call(
            kernel,
            out_shape=out_shape,
            grid_spec=pltpu.PrefetchScalarGridSpec(
                num_scalar_prefetch=4,
                grid=(capacity,),
                in_specs=[panel(0), panel(1), panel(0), panel(1), *other_specs],
                out_specs=out_specs,
            ),
            compiler_params=pltpu.CompilerParams(vmem_limit_bytes=48 * MIB),
            cost_estimate=pl.CostEstimate(
                flops=4 * capacity * virtual * virtual * (depth + virtual),
                bytes_accessed=8 * capacity * virtual * (depth + virtual),
                transcendentals=0,
            ),
        )(first, second, live, shift, *panels, *others)

    partial = []
    for part in range(passes):
        at = slice(part * depth, (part + 1) * depth)
        pieces = (factors, dressed) if passes == 1 else (factors[:, at], dressed[:, at])
        if partial:
            pieces = lax.optimization_barrier((*pieces, partial[-1]))
            partial[-1] = pieces[2]
        left_all, right_all = (whole.reshape(occupied, virtual, depth) for whole in gather(*pieces[:2]))
        panels = (left_all, right_all, right_all, left_all)
        if part < passes - 1:
            shape = (2, virtual, virtual)
            partial.append(run(
                partial_kernel, panels, (), (),
                jax.ShapeDtypeStruct((capacity,) + shape, jnp.float32), per_slot(*shape)))
    updated, energy = run(
        functools.partial(pair_kernel, len(partial)),
        panels,
        (amplitudes, off, level[:, None], level[None, :], *partial),
        [
            per_slot(virtual, virtual), fixed(virtual, virtual), fixed(virtual, 1), fixed(1, virtual),
            *[per_slot(2, virtual, virtual)] * len(partial),
        ],
        (
            jax.ShapeDtypeStruct(amplitudes.shape, jnp.float32),
            jax.ShapeDtypeStruct((capacity, 8, 128), jnp.float32),
        ),
        (per_slot(virtual, virtual), per_slot(8, 128)),
    )
    return updated, energy[:, 0, 0]


def solution(mesh):
    return jax.shard_map(
        local,
        mesh=mesh,
        in_specs=(
            P(("row", "col"), None),
            P(("col", "row"), None),
            P(("row", "col"), None, None),
            P(),
            P(),
            P(),
            P(),
        ),
        out_specs=(P(("row", "col"), None, None), P(("row", "col"))),
        check_vma=False,
    )
```

```python
import functools
import itertools

import jax
import jax.numpy as jnp
from jax import lax
from jax.experimental import pallas as pl
from jax.experimental.pallas import tpu as pltpu
from jax.sharding import PartitionSpec as P

MESH = pl.DeviceIdType.MESH
MIB = 1024 * 1024


def split_axis(size):
    return (size // 2, 2) if size % 2 == 0 else (size, 1)


def when(conds, body):
    if not conds:
        body()
        return
    total = conds[0]
    for extra in conds[1:]:
        total = jnp.logical_and(total, extra)
    pl.when(total)(body)


def neighbours(position, size):
    if size == 1:
        return []
    if size == 2:
        return [(0, 1 - position, [])]
    return [
        (0, position + 1, [position + 1 < size]),
        (1, position - 1, [position >= 1]),
    ]


def arrivals(position, size, step):
    if size == 2:
        return [(1 - position, None, [])]
    return [
        (position - step, 0, [position - step >= 0]),
        (position + step, 1, [position + step < size]),
    ]


def gather_kernel(row_count, col_count, routes, left_ref, right_ref, left_all, right_all, send_sem, recv_sem, own_sem):
    highs, lows = split_axis(row_count)
    lines, cores = split_axis(col_count)
    row, col = lax.axis_index("row"), lax.axis_index("col")
    high, low = row // lows, row % lows
    line, core = col // cores, col % cores
    place = {"line": line, "low": low, "high": high, "core": core}
    extent = {"line": lines, "low": lows, "high": highs, "core": cores}
    rows = left_ref.shape[0]
    share = rows * 2 // len(routes)
    arrays = [
        ((left_ref, right_ref)[side], (left_all, right_all)[side], side, part * share, order)
        for side, part, order in routes
    ]

    def device(at):
        return (at["high"] * lows + at["low"], at["line"] * cores + at["core"])

    def block_of(which, at):
        r, c = device(at)
        return r * col_count + c if arrays[which][2] == 0 else c * row_count + r

    def piece(which, blk):
        _, target, _, start, _ = arrays[which]
        return target.at[blk, pl.ds(start, share)]

    barrier = pltpu.get_barrier_semaphore()
    for axis in ("line", "low", "high", "core"):
        for _, other, conds in neighbours(place[axis], extent[axis]):
            when(conds, lambda axis=axis, other=other: pl.semaphore_signal(
                barrier, inc=1, device_id=device({**place, axis: other}), device_id_type=MESH))
    peers = 0
    for axis in ("line", "low", "high", "core"):
        for _, other, conds in neighbours(place[axis], extent[axis]):
            peers += conds[0].astype(jnp.int32) if conds else 1
    pl.semaphore_wait(barrier, peers)

    sent = []

    def plan(which, origin, stage, travel, guard, own=False):
        source, _, _, start, order = arrays[which]
        hops = []
        for later in range(stage, len(order)):
            axis = order[later]
            for way, other, conds in neighbours(place[axis], extent[axis]):
                if later == stage and not own and (extent[axis] == 2 or way != travel):
                    continue
                hops.append((axis, 2 * later + way, other, conds))
        for _, other, conds in neighbours(core, cores):
            hops.append(("core", 6, other, conds))
        copies = []
        for axis, lane, other, conds in hops:
            def make(axis=axis, lane=lane, other=other):
                blk = block_of(which, origin)
                return pltpu.make_async_remote_copy(
                    src_ref=source.at[pl.ds(start, share)] if own else piece(which, blk),
                    dst_ref=piece(which, blk),
                    send_sem=send_sem.at[which, blk, lane],
                    recv_sem=recv_sem.at[which, blk],
                    device_id=device({**place, axis: other}),
                    device_id_type=MESH,
                )

            copies.append((conds, make))
            sent.append((guard + conds, make))
        return copies

    def arrived(which, blk):
        pltpu.make_async_remote_copy(
            src_ref=piece(which, blk), dst_ref=piece(which, blk),
            send_sem=send_sem.at[which, blk, 0], recv_sem=recv_sem.at[which, blk],
            device_id=device(place), device_id_type=MESH,
        ).wait_recv()

    own_copies = []
    for which in range(len(arrays)):
        for conds, make in plan(which, place, 0, None, [], own=True):
            when(conds, lambda: make().start())
        source, _, _, start, _ = arrays[which]
        copy = pltpu.make_async_copy(
            source.at[pl.ds(start, share)], piece(which, block_of(which, place)), own_sem.at[which])
        copy.start()
        own_copies.append(copy)

    def take(which, origin, stage, travel, guard):
        copies = plan(which, origin, stage, travel, guard)

        def body():
            arrived(which, block_of(which, origin))
            for conds, make in copies:
                when(conds, lambda: make().start())

        when(guard, body)

    def reach(axis):
        near = [(0, place[axis], None, [])]
        for step in range(1, extent[axis]):
            near += [(step, *arrival) for arrival in arrivals(place[axis], extent[axis], step)]
        return near

    takes = []
    for which in range(len(arrays)):
        order = arrays[which][4]
        for ways in itertools.product(*(reach(axis) for axis in order)):
            hops = sum(way[0] for way in ways)
            if hops == 0:
                continue
            stage = max(k for k in range(len(order)) if ways[k][0] > 0)
            origin = {**place, **{axis: way[1] for axis, way in zip(order, ways)}}
            guard = [cond for way in ways for cond in way[3]]
            takes.append((hops, stage, len(takes), which, origin, ways[stage][2], guard))
    for _, stage, _, which, origin, travel, guard in sorted(takes, key=lambda entry: entry[:3]):
        take(which, origin, stage, travel, guard)

    if cores > 1:
        def from_sibling(index, carry):
            at = {
                "high": index // (lows * lines),
                "low": index // lines % lows,
                "line": index % lines,
                "core": 1 - core,
            }
            for which in range(len(arrays)):
                arrived(which, block_of(which, at))
            return carry

        lax.fori_loop(0, highs * lows * lines, from_sibling, 0)
    for conds, make in sent:
        when(conds, lambda: make().wait_send())
    for copy in own_copies:
        copy.wait()


def gather(factors, dressed):
    row_count, col_count = lax.axis_size("row"), lax.axis_size("col")
    devices = row_count * col_count
    rows, depth = factors.shape
    whole = jax.ShapeDtypeStruct((devices, rows, depth), factors.dtype)
    routes = [(0, 0, ("line", "low", "high")), (1, 0, ("line", "high", "low"))]
    if rows % 32 == 0 and devices <= 32:
        routes += [(0, 1, ("low", "line", "high")), (1, 1, ("high", "line", "low"))]
    return pl.pallas_call(
        functools.partial(gather_kernel, row_count, col_count, tuple(routes)),
        out_shape=(whole, whole),
        in_specs=[pl.BlockSpec(memory_space=pl.ANY)] * 2,
        out_specs=(pl.BlockSpec(memory_space=pl.ANY), pl.BlockSpec(memory_space=pl.ANY)),
        scratch_shapes=[
            pltpu.SemaphoreType.DMA((len(routes), devices, 7)),
            pltpu.SemaphoreType.DMA((len(routes), devices)),
            pltpu.SemaphoreType.DMA((len(routes),)),
        ],
        compiler_params=pltpu.CompilerParams(
            collective_id=0, has_side_effects=True, vmem_limit_bytes=4 * MIB
        ),
    )(factors, dressed)


def products(l_i, y_j, y_i, l_j):
    contract = (((1,), (1,)), ((), ()))
    forward = lax.dot_general(l_i[0], y_j[0], contract, preferred_element_type=jnp.float32)
    backward = lax.dot_general(y_i[0], l_j[0], contract, preferred_element_type=jnp.float32)
    return forward, backward


def partial_kernel(first, second, live, shift, l_i, y_j, y_i, l_j, sums):
    forward, backward = products(l_i, y_j, y_i, l_j)
    sums[0, 0] = forward
    sums[0, 1] = backward


def pair_kernel(earlier, first, second, live, shift, l_i, y_j, y_i, l_j, amp, coupling, level_col, level_row, *rest):
    out, energy = rest[earlier:]
    slot = pl.program_id(0)
    forward, backward = products(l_i, y_j, y_i, l_j)
    for sums in rest[:earlier]:
        forward = forward + sums[0, 0]
        backward = backward + sums[0, 1]
    apart = forward.astype(jnp.bfloat16).astype(jnp.float32) + backward.astype(jnp.bfloat16).astype(jnp.float32)
    same = first[slot] == second[slot]
    source = jnp.where(same, forward + backward, apart).astype(jnp.bfloat16).astype(jnp.float32)
    current = amp[0].astype(jnp.bfloat16)
    mixed = jnp.dot(coupling[...], current, preferred_element_type=jnp.float32)
    mixed = mixed + jnp.dot(current, coupling[...], preferred_element_type=jnp.float32)
    denominator = level_col[...] + level_row[...] - shift[slot]
    updated = jnp.where(live[slot] > 0, -(source + mixed) / denominator, 0.0)
    out[0] = updated
    total = jnp.sum(source * updated) / (updated.shape[0] * updated.shape[1])
    energy[...] = jnp.full(energy.shape, total, jnp.float32)


def local(factors, dressed, amplitudes, fock_vv, occ_energy, pair_list, owner_map):
    col_count = lax.axis_size("col")
    capacity = amplitudes.shape[0]
    virtual = fock_vv.shape[0]
    occupied = occ_energy.shape[0]
    depth = factors.shape[1]
    passes = 1 if lax.axis_size("row") * col_count <= 32 else 2
    depth = depth // passes

    own_index = lax.axis_index("row") * col_count + lax.axis_index("col")
    positions = jnp.arange(pair_list.shape[0], dtype=jnp.int32)
    mine = owner_map == own_index
    rank = jnp.sum((mine[None, :] & (positions[:, None] > positions[None, :])).astype(jnp.int32), axis=1)
    hit = mine[None, :] & (rank[None, :] == jnp.arange(capacity, dtype=jnp.int32)[:, None])
    live = jnp.sum(hit.astype(jnp.int32), axis=1)
    pair_orbs = jnp.sum(jnp.where(hit[:, :, None], pair_list[None, :, :], 0), axis=1)
    first, second = pair_orbs[:, 0], pair_orbs[:, 1]
    shift = occ_energy[first] + occ_energy[second]

    on_diagonal = jnp.eye(virtual, dtype=jnp.bool_)
    level = jnp.sum(jnp.where(on_diagonal, fock_vv, 0.0), axis=0)
    off = jnp.where(on_diagonal, 0.0, fock_vv).astype(jnp.bfloat16)

    def panel(pick):
        return pl.BlockSpec((1, virtual, depth), lambda s, f, g, *_: ((f, g)[pick][s], 0, 0))

    def fixed(*shape):
        return pl.BlockSpec(shape, lambda s, *_: (0,) * len(shape))

    def per_slot(*shape):
        return pl.BlockSpec((1,) + shape, lambda s, *_: (s,) + (0,) * len(shape))

    def run(kernel, panels, others, other_specs, out_shape, out_specs):
        return pl.pallas_call(
            kernel,
            out_shape=out_shape,
            grid_spec=pltpu.PrefetchScalarGridSpec(
                num_scalar_prefetch=4,
                grid=(capacity,),
                in_specs=[panel(0), panel(1), panel(0), panel(1), *other_specs],
                out_specs=out_specs,
            ),
            compiler_params=pltpu.CompilerParams(vmem_limit_bytes=48 * MIB),
            cost_estimate=pl.CostEstimate(
                flops=4 * capacity * virtual * virtual * (depth + virtual),
                bytes_accessed=8 * capacity * virtual * (depth + virtual),
                transcendentals=0,
            ),
        )(first, second, live, shift, *panels, *others)

    partial = []
    for part in range(passes):
        at = slice(part * depth, (part + 1) * depth)
        pieces = (factors, dressed) if passes == 1 else (factors[:, at], dressed[:, at])
        if partial:
            pieces = lax.optimization_barrier((*pieces, partial[-1]))
            partial[-1] = pieces[2]
        left_all, right_all = (whole.reshape(occupied, virtual, depth) for whole in gather(*pieces[:2]))
        panels = (left_all, right_all, right_all, left_all)
        if part < passes - 1:
            shape = (2, virtual, virtual)
            partial.append(run(
                partial_kernel, panels, (), (),
                jax.ShapeDtypeStruct((capacity,) + shape, jnp.float32), per_slot(*shape)))
    updated, energy = run(
        functools.partial(pair_kernel, len(partial)),
        panels,
        (amplitudes, off, level[:, None], level[None, :], *partial),
        [
            per_slot(virtual, virtual), fixed(virtual, virtual), fixed(virtual, 1), fixed(1, virtual),
            *[per_slot(2, virtual, virtual)] * len(partial),
        ],
        (
            jax.ShapeDtypeStruct(amplitudes.shape, jnp.float32),
            jax.ShapeDtypeStruct((capacity, 8, 128), jnp.float32),
        ),
        (per_slot(virtual, virtual), per_slot(8, 128)),
    )
    return updated, energy[:, 0, 0]


def solution(mesh):
    return jax.shard_map(
        local,
        mesh=mesh,
        in_specs=(
            P(("row", "col"), None),
            P(("col", "row"), None),
            P(("row", "col"), None, None),
            P(),
            P(),
            P(),
            P(),
        ),
        out_specs=(P(("row", "col"), None, None), P(("row", "col"))),
        check_vma=False,
    )
```
